128 devices in a mesh: row: 8 (over x_hi, y), col: 16 (over x_lo, z, core).
Axes of the slice: x: 4 (x_hi: 2, x_lo: 2; x = x_hi * 2 + x_lo), y: 4, z: 4, core: 2. Of those that a mesh axis runs over, the one named last changes fastest.
Arguments:
- grad_out: bfloat16 [1024, 16384], P('col', 'row'), may hold values from -6 to 6
- gate: bfloat16 [1024, 26624], P('row', 'col'), may hold values from -8 to 8
- up: bfloat16 [1024, 26624], P('row', 'col'), may hold values from -6 to 6
- w_down: bfloat16 [16384, 26624], P('row', 'col'), may hold values from -0.046875 to 0.046875
Outputs:
- grad_gate: bfloat16 [1024, 26624], P('row', 'col')
- grad_up: bfloat16 [1024, 26624], P('row', 'col')
- grad_weight: bfloat16 [16384, 26624], P('row', 'col')
The draws below stay inside these ranges and needn't reach their ends.
All inputs are finite; a program needn't handle non-finite values.
Results may differ from the reference program's by a relative error of at most 0.0049.
Values may be sent and summed in bfloat16 or wider, within the bound.
A program may use at most 128 MiB of HBM per device.

```python
import jax
import jax.numpy as jnp
from jax import lax

D = 16384
FF = 26624
TOKENS = 1024


def block_levels(rng, extent, pieces, low, high):
    level = 1.0
    for position, parts in pieces:
        steps = jax.random.uniform(jax.random.fold_in(jax.random.fold_in(rng, 6), position), (parts,), jnp.float32, low / len(pieces), high / len(pieces))
        level = level * jnp.repeat(jnp.exp(steps), extent[position] // parts).reshape((-1,) + (1,) * (len(extent) - 1 - position))
    return level


def normal_values(key, shape, spread, reach, pieces=(), held_as=jnp.bfloat16):
    gain = block_levels(key, shape, pieces, -0.22, 0.18) if pieces else 1.0
    result = jax.random.normal(key, shape, jnp.float32) * spread * gain
    return jnp.minimum(jnp.maximum(result, -reach), reach).astype(held_as)


def setup_inputs(seed: int = 0) -> dict:
    seeds = jax.random.split(jax.random.key(seed), 5)
    return {
        "grad_out": normal_values(seeds[0], (TOKENS, D), 1.0, 6.0, ((0, 16), (1, 8))),
        "gate": normal_values(seeds[1], (TOKENS, FF), 2.0, 8.0, ((0, 8), (1, 16))),
        "up": normal_values(seeds[2], (TOKENS, FF), 1.0, 6.0, ((0, 8), (1, 16))),
        "w_down": normal_values(seeds[3], (D, FF), D ** -0.5, 0.046875, ((0, 8), (1, 16))),
    }


def reference(grad_out, gate, up, w_down):
    grad_hidden = jnp.dot(grad_out, w_down, preferred_element_type=jnp.float32)
    gate_f = gate.astype(jnp.float32)
    up_f = up.astype(jnp.float32)
    sig = jax.nn.sigmoid(gate_f)
    silu = gate_f * sig
    hidden = (silu * up_f).astype(jnp.bfloat16)
    grad_up = (grad_hidden * silu).astype(jnp.bfloat16)
    grad_gate = (grad_hidden * up_f * sig * (1.0 + gate_f * (1.0 - sig))).astype(jnp.bfloat16)
    grad_weight = lax.dot_general(grad_out, hidden, (((0,), (0,)), ((), ())), preferred_element_type=jnp.float32)
    return grad_gate, grad_up, grad_weight.astype(jnp.bfloat16)
```

```python
import functools

import jax
import jax.numpy as jnp
from jax import lax
from jax.experimental import pallas as pl
from jax.experimental.pallas import tpu as pltpu
from jax.sharding import PartitionSpec as P

MESH = pl.DeviceIdType.MESH
BF16, F32 = jnp.bfloat16, jnp.float32
NY, NX = 4, 2
COPIES = 96


def kernel(
    split, go_in, gate_in, up_in, w_in, gg_out, gu_out, gw_out,
    go, w, acc, hid, gate, up, silu, slope, gw, gg, gu,
    pfar, pnear, px, qx, qfar, qnear, local, ssem, rsem,
):
    tokens, units = hid.shape
    features = go.shape[1]
    own = tokens // (NX * NY)
    half, part = own // 2, own // 2
    group = NX * own
    row, col = lax.axis_index("row"), lax.axis_index("col")
    xh, y = row // NY, row % NY
    xl, z, c = col // (2 * NY), (col // 2) % NY, col % 2
    yp, ym, yf = (y + 1) % NY, (y + 3) % NY, (y + 2) % NY
    zp, zm, zf = (z + 1) % NY, (z + 3) % NY, (z + 2) % NY
    up_y, dn_y, over_x = (xh * NY + yp, col), (xh * NY + ym, col), ((1 - xh) * NY + y, col)

    def at_col(a, b, d):
        return (row, a * (2 * NY) + b * 2 + d)

    up_z, dn_z = at_col(xl, zp, c), at_col(xl, zm, c)
    next_x, other = at_col(1 - xl, z, c), at_col(xl, z, 1 - c)
    peers = (up_y, dn_y, over_x, up_z, dn_z, next_x, other)

    cols = (pl.ds(0, split), pl.ds(split, units - split))

    def rows(a, b, h=None):
        start = b * group + a * own
        if h is None:
            return pl.ds(pl.multiple_of(start, own), own)
        return pl.ds(pl.multiple_of(start + h * half, half), half)

    def panel(a, b, d, h=None):
        start = b * group + a * own + d * part
        if h is None:
            return pl.ds(pl.multiple_of(start, part), part)
        return pl.ds(pl.multiple_of(start + h * (part // 2), part // 2), part // 2)

    names, sent = {}, []

    def index(name):
        return names.setdefault(name, len(names))

    def send(name, src, dst, device):
        k = index(name)
        copy = pltpu.make_async_remote_copy(src, dst, ssem.at[k], rsem.at[k], device_id=device, device_id_type=MESH)
        copy.start()
        sent.append(copy)

    def arrived(name, dst):
        k = index(name)
        pltpu.make_async_remote_copy(dst, dst, ssem.at[k], rsem.at[k], device_id=other, device_id_type=MESH).wait_recv()

    loads = [
        pltpu.make_async_copy(gate_in, gate, local.at[0]),
        pltpu.make_async_copy(up_in, up, local.at[1]),
        pltpu.make_async_copy(go_in, go.at[panel(xl, z, c)], local.at[2]),
        pltpu.make_async_copy(w_in, w, local.at[3]),
    ]
    for load in loads:
        load.start()
    barrier = pltpu.get_barrier_semaphore()
    for peer in peers:
        pl.semaphore_signal(barrier, inc=1, device_id=peer, device_id_type=MESH)
    pl.semaphore_wait(barrier, len(peers))

    def gsend(name, a, b, d, device, h=None, src=None):
        ref = go.at[panel(a, b, d, h)]
        send(name, ref if src is None else src, ref, device)

    def garrived(name, a, b, d, h=None):
        arrived(name, go.at[panel(a, b, d, h)])

    gsend("g_next", xl, z, c, next_x, src=go_in)
    gsend("g_up", xl, z, c, up_z, src=go_in)
    gsend("g_dn", xl, z, c, dn_z, src=go_in)
    gsend("g_other", xl, z, c, other, src=go_in)

    def hsend(name, a, b, p, device, h):
        ref = hid.at[rows(a, b, h), cols[p]]
        send((name, p, h), ref, ref, device)

    def harrived(name, a, b, p, h):
        arrived((name, p, h), hid.at[rows(a, b, h), cols[p]])

    def activate(p, h):
        step = 16

        @pl.loop(0, half // step)
        def _(i):
            at = pl.ds(pl.multiple_of(h * half + i * step, step), step)
            to = pl.ds(pl.multiple_of(y * group + xh * own + h * half + i * step, step), step)
            v, u = gate[at, cols[p]].astype(F32), up[at, cols[p]].astype(F32)
            s = jax.nn.sigmoid(v)
            act = v * s
            silu[at, cols[p]] = act
            slope[at, cols[p]] = u * s * (1.0 + v * (1.0 - s))
            hid[to, cols[p]] = (act * u).astype(BF16)

    loads[0].wait()
    loads[1].wait()
    for p in (1, 0):
        activate(p, 0)
        hsend("h_up", xh, y, p, up_y, 0)
        activate(p, 1)
        hsend("h_dn", xh, y, p, dn_y, 1)
        hsend("h_up", xh, y, p, up_y, 1)
        hsend("h_dn", xh, y, p, dn_y, 0)
        if p == 0:
            for q in (0, 1):
                for h in (0, 1):
                    hsend("h_x", xh, y, q, over_x, h)

    def near_h(p):
        harrived("h_up", xh, ym, p, 0)
        hsend("h_up2", xh, ym, p, up_y, 0)
        harrived("h_dn", xh, yp, p, 1)
        hsend("h_dn2", xh, yp, p, dn_y, 1)
        harrived("h_up", xh, ym, p, 1)
        harrived("h_dn", xh, yp, p, 0)
        if p == 1:
            for h in (0, 1):
                hsend("h_xm", xh, ym, p, over_x, h)
                hsend("h_xp", xh, yp, p, over_x, h)

    def project(b):
        at = pl.ds(pl.multiple_of(b * group, group), group)
        wide = 256

        @pl.loop(0, units // wide)
        def _(j):
            to = pl.ds(pl.multiple_of(j * wide, wide), wide)
            acc[at, to] = jnp.dot(go[at, :], w[:, to], preferred_element_type=F32).astype(BF16)

        rest = units % wide
        if rest:
            to = pl.ds(units - rest, rest)
            acc[at, to] = jnp.dot(go[at, :], w[:, to], preferred_element_type=F32).astype(BF16)

    near_h(1)
    garrived("g_next", 1 - xl, z, c)
    gsend("g_xup", 1 - xl, z, c, up_z)
    gsend("g_xdn", 1 - xl, z, c, dn_z)
    gsend("g_xother", 1 - xl, z, c, other)
    garrived("g_up", xl, zm, c)
    gsend("g_up2", xl, zm, c, up_z, 0)
    gsend("g_upo", xl, zm, c, other)
    garrived("g_dn", xl, zp, c)
    gsend("g_dn2", xl, zp, c, dn_z, 1)
    gsend("g_dno", xl, zp, c, other)
    loads[2].wait()
    loads[3].wait()
    garrived("g_other", xl, z, 1 - c)
    garrived("g_xother", 1 - xl, z, 1 - c)
    project(z)
    near_h(0)
    for h in (0, 1):
        harrived("h_x", 1 - xh, y, 0, h)
    hsend("h_gup", 1 - xh, y, 0, up_y, 0)
    hsend("h_gdn", 1 - xh, y, 0, dn_y, 1)
    hsend("h_gup", 1 - xh, y, 0, up_y, 1)
    hsend("h_gdn", 1 - xh, y, 0, dn_y, 0)
    garrived("g_xup", 1 - xl, zm, c)
    gsend("g_xup2", 1 - xl, zm, c, up_z, 0)
    gsend("g_xupo", 1 - xl, zm, c, other)
    garrived("g_xdn", 1 - xl, zp, c)
    gsend("g_xdn2", 1 - xl, zp, c, dn_z, 1)
    gsend("g_xdno", 1 - xl, zp, c, other)
    harrived("h_up2", xh, yf, 1, 0)
    hsend("h_xf", xh, yf, 1, over_x, 0)
    harrived("h_dn2", xh, yf, 1, 1)
    hsend("h_xf", xh, yf, 1, over_x, 1)
    garrived("g_upo", xl, zm, 1 - c)
    garrived("g_xupo", 1 - xl, zm, 1 - c)
    project(zm)
    garrived("g_up2", xl, zf, c, 0)
    garrived("g_dn2", xl, zf, c, 1)
    gsend("g_faro", xl, zf, c, other)
    garrived("g_dno", xl, zp, 1 - c)
    garrived("g_xdno", 1 - xl, zp, 1 - c)
    project(zp)
    garrived("g_xup2", 1 - xl, zf, c, 0)
    garrived("g_xdn2", 1 - xl, zf, c, 1)
    gsend("g_xfaro", 1 - xl, zf, c, other)
    harrived("h_gup", 1 - xh, ym, 0, 0)
    hsend("h_gup2", 1 - xh, ym, 0, up_y, 0)
    harrived("h_gdn", 1 - xh, yp, 0, 1)
    hsend("h_gdn2", 1 - xh, yp, 0, dn_y, 1)
    garrived("g_faro", xl, zf, 1 - c)
    garrived("g_xfaro", 1 - xl, zf, 1 - c)
    project(zf)

    sides = (1 - xh, xh)
    order = (yf, yp, ym, y)
    for i, b in enumerate(order):
        send(("q_x", i), acc.at[rows(1 - xh, b), cols[1]], qx.at[i], over_x)
    for s in (0, 1):
        send(("p_far_up", s), acc.at[rows(sides[s], yf, 0), cols[0]], pfar.at[s, 0], up_y)
        send(("p_far_dn", s), acc.at[rows(sides[s], yf, 1), cols[0]], pfar.at[s, 1], dn_y)

    def pnear_to(d, s, h):
        name, b, device = (("p_up", yp, up_y), ("p_dn", ym, dn_y))[d]
        send((name, s, h), acc.at[rows(sides[s], b, h), cols[0]], pnear.at[s, d, pl.ds(h * half, half)], device)

    for s in (0, 1):
        pnear_to(0, s, 1)
        pnear_to(1, s, 0)

    def add(at, p, ref):
        acc[at, cols[p]] = (acc[at, cols[p]].astype(F32) + ref[...].astype(F32)).astype(BF16)

    def meet(s):
        for d, (name, b) in enumerate((("p_far_up", yp), ("p_far_dn", ym))):
            arrived((name, s), pfar.at[s, d])
            add(rows(sides[s], b, d), 0, pfar.at[s, d])
            pnear_to(d, s, d)

    stores = []

    def outer(f):
        deep = features // 4
        at = pl.ds(f * deep, deep)
        for start, wide in ((0, 512), (512, 512), (1024, 640)):
            to = pl.ds(start, wide)
            gw[at, to] = lax.dot_general(
                go[:, at], hid[:, to], (((0,), (0,)), ((), ())), preferred_element_type=F32
            ).astype(BF16)
        store = pltpu.make_async_copy(gw.at[at], gw_out.at[at], local.at[4 + f])
        store.start()
        stores.append(store)

    for p in (0, 1):
        for h in (0, 1):
            if p == 1:
                harrived("h_x", 1 - xh, y, 1, h)
                harrived("h_xm", 1 - xh, ym, 1, h)
                harrived("h_xp", 1 - xh, yp, 1, h)
                harrived("h_xf", 1 - xh, yf, 1, h)
    harrived("h_up2", xh, yf, 0, 0)
    harrived("h_dn2", xh, yf, 0, 1)
    harrived("h_gup", 1 - xh, ym, 0, 1)
    harrived("h_gdn", 1 - xh, yp, 0, 0)
    harrived("h_gup2", 1 - xh, yf, 0, 0)
    harrived("h_gdn2", 1 - xh, yf, 0, 1)
    outer(0)
    meet(0)
    outer(1)
    meet(1)
    outer(2)

    def qadd(i):
        arrived(("q_x", i), qx.at[i])
        add(rows(xh, order[i]), 1, qx.at[i])

    def qnear_to(d, h):
        name, b, device = (("q_up", yp, up_y), ("q_dn", ym, dn_y))[d]
        send((name, h), acc.at[rows(xh, b, h), cols[1]], qnear.at[d, pl.ds(h * half, half)], device)

    qadd(0)
    send("q_far_up", acc.at[rows(xh, yf, 0), cols[1]], qfar.at[0], up_y)
    send("q_far_dn", acc.at[rows(xh, yf, 1), cols[1]], qfar.at[1], dn_y)
    outer(3)
    qadd(1)
    qnear_to(0, 1)
    qadd(2)
    qnear_to(1, 0)
    for d, (name, b) in enumerate((("q_far_up", yp), ("q_far_dn", ym))):
        arrived(name, qfar.at[d])
        add(rows(xh, b, d), 1, qfar.at[d])
        qnear_to(d, d)

    def near_sum(s):
        for h in (0, 1):
            arrived(("p_up", s, h), pnear.at[s, 0, pl.ds(h * half, half)])
            arrived(("p_dn", s, h), pnear.at[s, 1, pl.ds(h * half, half)])

    near_sum(0)
    for h in (0, 1):
        at, piece = rows(1 - xh, y, h), pl.ds(h * half, half)
        total = acc[at, cols[0]].astype(F32) + pnear[0, 0, piece].astype(F32) + pnear[0, 1, piece].astype(F32)
        acc[at, cols[0]] = total.astype(BF16)
        send(("p_x", h), acc.at[at, cols[0]], px.at[piece], over_x)
    qadd(3)

    def finish(p, piece, total):
        gu[piece, cols[p]] = (total * silu[piece, cols[p]]).astype(BF16)
        gg[piece, cols[p]] = (total * slope[piece, cols[p]]).astype(BF16)

    near_sum(1)
    for h in (0, 1):
        piece = pl.ds(h * half, half)
        arrived(("p_x", h), px.at[piece])
        total = acc[rows(xh, y, h), cols[0]].astype(F32) + px[piece].astype(F32)
        total = total + pnear[1, 0, piece].astype(F32) + pnear[1, 1, piece].astype(F32)
        finish(0, piece, total)
    for h in (0, 1):
        piece = pl.ds(h * half, half)
        arrived(("q_up", h), qnear.at[0, piece])
        arrived(("q_dn", h), qnear.at[1, piece])
        total = acc[rows(xh, y, h), cols[1]].astype(F32)
        total = total + qnear[0, piece].astype(F32) + qnear[1, piece].astype(F32)
        finish(1, piece, total)
    stores.append(pltpu.make_async_copy(gg, gg_out, local.at[8]))
    stores.append(pltpu.make_async_copy(gu, gu_out, local.at[9]))
    stores[-1].start()
    stores[-2].start()
    for copy in sent:
        copy.wait_send()
    for store in stores:
        store.wait()


def on_device(grad_out, gate, up, w_down):
    own, units = gate.shape
    features = w_down.shape[0]
    tokens = own * NX * NY
    split = 1024
    rest = units - split
    half = own // 2
    anywhere = pl.BlockSpec(memory_space=pl.ANY)
    return pl.pallas_call(
        functools.partial(kernel, split),
        out_shape=(
            jax.ShapeDtypeStruct((own, units), BF16),
            jax.ShapeDtypeStruct((own, units), BF16),
            jax.ShapeDtypeStruct((features, units), BF16),
        ),
        in_specs=[anywhere] * 4,
        out_specs=(anywhere,) * 3,
        scratch_shapes=[
            pltpu.VMEM((tokens, features), BF16),
            pltpu.VMEM((features, units), BF16),
            pltpu.VMEM((tokens, units), BF16),
            pltpu.VMEM((tokens, units), BF16),
            pltpu.VMEM((own, units), BF16),
            pltpu.VMEM((own, units), BF16),
            pltpu.VMEM((own, units), F32),
            pltpu.VMEM((own, units), F32),
            pltpu.VMEM((features, units), BF16),
            pltpu.VMEM((own, units), BF16),
            pltpu.VMEM((own, units), BF16),
            pltpu.VMEM((2, 2, half, split), BF16),
            pltpu.VMEM((2, 2, own, split), BF16),
            pltpu.VMEM((own, split), BF16),
            pltpu.VMEM((NY, own, rest), BF16),
            pltpu.VMEM((2, half, rest), BF16),
            pltpu.VMEM((2, own, rest), BF16),
            pltpu.SemaphoreType.DMA((10,)),
            pltpu.SemaphoreType.DMA((COPIES,)),
            pltpu.SemaphoreType.DMA((COPIES,)),
        ],
        compiler_params=pltpu.CompilerParams(
            collective_id=0, has_side_effects=True, vmem_limit_bytes=56 * 2**20
        ),
        cost_estimate=pl.CostEstimate(
            flops=4 * tokens * features * units, bytes_accessed=4 * features * units, transcendentals=own * units
        ),
    )(grad_out, gate, up, w_down)


def solution(mesh):
    return jax.shard_map(
        on_device,
        mesh=mesh,
        in_specs=(P("col", "row"), P("row", "col"), P("row", "col"), P("row", "col")),
        out_specs=(P("row", "col"),) * 3,
        check_vma=False,
    )
```

```python
import functools

import jax
import jax.numpy as jnp
from jax import lax
from jax.experimental import pallas as pl
from jax.experimental.pallas import tpu as pltpu
from jax.sharding import PartitionSpec as P

MESH = pl.DeviceIdType.MESH
BF16, F32 = jnp.bfloat16, jnp.float32
NY, NX = 4, 2
COPIES = 96


def kernel(
    hsplit, rsplit, go_in, gate_in, up_in, w_in, gg_out, gu_out, gw_out,
    go, w, acc, hid, gate, up, silu, slope, gw, gg, gu,
    pfar, pnear, px, qx, qfar, qnear, local, ssem, rsem,
):
    tokens, units = hid.shape
    features = go.shape[1]
    own = tokens // (NX * NY)
    half, part = own // 2, own // 2
    group = NX * own
    row, col = lax.axis_index("row"), lax.axis_index("col")
    xh, y = row // NY, row % NY
    xl, z, c = col // (2 * NY), (col // 2) % NY, col % 2
    yp, ym, yf = (y + 1) % NY, (y + 3) % NY, (y + 2) % NY
    zp, zm, zf = (z + 1) % NY, (z + 3) % NY, (z + 2) % NY
    up_y, dn_y, over_x = (xh * NY + yp, col), (xh * NY + ym, col), ((1 - xh) * NY + y, col)

    def at_col(a, b, d):
        return (row, a * (2 * NY) + b * 2 + d)

    up_z, dn_z = at_col(xl, zp, c), at_col(xl, zm, c)
    next_x, other = at_col(1 - xl, z, c), at_col(xl, z, 1 - c)
    peers = (up_y, dn_y, over_x, up_z, dn_z, next_x, other)

    hcols = (pl.ds(0, hsplit), pl.ds(hsplit, units - hsplit))
    rcols = (pl.ds(0, rsplit), pl.ds(rsplit, units - rsplit))

    def rows(a, b, h=None):
        start = b * group + a * own
        if h is None:
            return pl.ds(pl.multiple_of(start, own), own)
        return pl.ds(pl.multiple_of(start + h * half, half), half)

    def panel(a, b, d, h=None):
        start = b * group + a * own + d * part
        if h is None:
            return pl.ds(pl.multiple_of(start, part), part)
        return pl.ds(pl.multiple_of(start + h * (part // 2), part // 2), part // 2)

    names, sent = {}, {}

    def index(name):
        return names.setdefault(name, len(names))

    def send(name, src, dst, device, note=True):
        k = index(name)
        if note:
            sent[name] = dst
        pltpu.make_async_remote_copy(src, dst, ssem.at[k], rsem.at[k], device_id=device, device_id_type=MESH).start()

    def drain():
        for name, ref in sent.items():
            k = index(name)
            pltpu.make_async_remote_copy(ref, ref, ssem.at[k], rsem.at[k], device_id=other, device_id_type=MESH).wait_send()
        sent.clear()

    def arrived(name, dst):
        k = index(name)
        pltpu.make_async_remote_copy(dst, dst, ssem.at[k], rsem.at[k], device_id=other, device_id_type=MESH).wait_recv()

    loads = [
        pltpu.make_async_copy(gate_in, gate, local.at[0]),
        pltpu.make_async_copy(up_in, up, local.at[1]),
        pltpu.make_async_copy(go_in, go.at[panel(xl, z, c)], local.at[2]),
        pltpu.make_async_copy(w_in, w, local.at[3]),
    ]
    barrier = pltpu.get_barrier_semaphore()
    for peer in peers:
        pl.semaphore_signal(barrier, inc=1, device_id=peer, device_id_type=MESH)
    for load in loads[:3]:
        load.start()

    def gsend(name, a, b, d, device, h=None, src=None):
        ref = go.at[panel(a, b, d, h)]
        send((name, h), ref if src is None else src, ref, device)

    def garrived(name, a, b, d, h=None):
        arrived((name, h), go.at[panel(a, b, d, h)])

    def hsend(name, a, b, p, device, h):
        ref = hid.at[rows(a, b, h), hcols[p]]
        send((name, p, h), ref, ref, device)

    def harrived(name, a, b, p, h):
        arrived((name, p, h), hid.at[rows(a, b, h), hcols[p]])

    def activate(p, h):
        step = 16

        @pl.loop(0, half // step)
        def _(i):
            at = pl.ds(pl.multiple_of(h * half + i * step, step), step)
            to = pl.ds(pl.multiple_of(y * group + xh * own + h * half + i * step, step), step)
            v, u = gate[at, hcols[p]].astype(F32), up[at, hcols[p]].astype(F32)
            s = jax.nn.sigmoid(v)
            act = v * s
            silu[at, hcols[p]] = act
            slope[at, hcols[p]] = u * s * (1.0 + v * (1.0 - s))
            hid[to, hcols[p]] = (act * u).astype(BF16)

    loads[0].wait()
    loads[1].wait()
    loads[3].start()
    for p in (0, 1):
        for h in (0, 1):
            activate(p, h)
    pl.semaphore_wait(barrier, len(peers))
    pieces = [go_in.at[pl.ds(h * (part // 2), part // 2)] for h in (0, 1)]
    for h in (0, 1):
        gsend("g_next", xl, z, c, next_x, h, pieces[h])
        gsend("g_up", xl, z, c, up_z, h, pieces[h])
        gsend("g_dn", xl, z, c, dn_z, 1 - h, pieces[1 - h])
        hsend("h_up", xh, y, 0, up_y, h)
        hsend("h_dn", xh, y, 0, dn_y, 1 - h)
        hsend("h_x", xh, y, 0, over_x, h)
    for h in (0, 1):
        hsend("h_up", xh, y, 1, up_y, h)
        hsend("h_dn", xh, y, 1, dn_y, 1 - h)
        hsend("h_x", xh, y, 1, over_x, h)
    gsend("g_other", xl, z, c, other, src=go_in)

    def project(b):
        at = pl.ds(pl.multiple_of(b * group, group), group)
        wide = 256

        @pl.loop(0, units // wide)
        def _(j):
            to = pl.ds(pl.multiple_of(j * wide, wide), wide)
            acc[at, to] = jnp.dot(go[at, :], w[:, to], preferred_element_type=F32).astype(BF16)

        rest = units % wide
        if rest:
            to = pl.ds(units - rest, rest)
            acc[at, to] = jnp.dot(go[at, :], w[:, to], preferred_element_type=F32).astype(BF16)

    sides = (1 - xh, xh)
    order = (z, zm, zp, zf)

    def pfar_to(s, d):
        name, device = (("p_far_up", up_y), ("p_far_dn", dn_y))[d]
        send((name, s), acc.at[rows(sides[s], yf, d), rcols[0]], pfar.at[s, d], device, False)

    def pnear_to(s, d, h):
        name, b, device = (("p_up", yp, up_y), ("p_dn", ym, dn_y))[d]
        to = pnear.at[s, d, pl.ds(h * half, half)]
        send((name, s, h), acc.at[rows(sides[s], b, h), rcols[0]], to, device, False)

    def release(i):
        send(("q_x", i), acc.at[rows(1 - xh, order[i]), rcols[1]], qx.at[i], over_x)
        away = (order[i] - y + NY) % NY

        @pl.when(away == 2)
        def _():
            for s in (0, 1):
                pfar_to(s, 0)
                pfar_to(s, 1)

        @pl.when(away == 1)
        def _():
            for s in (0, 1):
                pnear_to(s, 0, 1)

        @pl.when(away == 3)
        def _():
            for s in (0, 1):
                pnear_to(s, 1, 0)

    for h in (0, 1):
        garrived("g_next", 1 - xl, z, c, h)
        gsend("g_xup", 1 - xl, z, c, up_z, h)
        gsend("g_xdn", 1 - xl, z, c, dn_z, h)
        gsend("g_xother", 1 - xl, z, c, other, h)
        if h == 0:
            harrived("h_up", xh, ym, 0, 0)
            hsend("h_up2", xh, ym, 0, up_y, 0)
            harrived("h_dn", xh, yp, 0, 1)
            hsend("h_dn2", xh, yp, 0, dn_y, 1)
    garrived("g_up", xl, zm, c, 0)
    gsend("g_up2", xl, zm, c, up_z, 0)
    garrived("g_dn", xl, zp, c, 1)
    gsend("g_dn2", xl, zp, c, dn_z, 1)
    garrived("g_up", xl, zm, c, 1)
    gsend("g_upo", xl, zm, c, other)
    garrived("g_dn", xl, zp, c, 0)
    gsend("g_dno", xl, zp, c, other)
    harrived("h_x", 1 - xh, y, 0, 0)
    hsend("h_gup", 1 - xh, y, 0, up_y, 0)
    hsend("h_gdn", 1 - xh, y, 0, dn_y, 0)
    harrived("h_up", xh, ym, 1, 0)
    hsend("h_up2", xh, ym, 1, up_y, 0)
    hsend("h_xm", xh, ym, 1, over_x, 0)
    harrived("h_dn", xh, yp, 1, 1)
    hsend("h_dn2", xh, yp, 1, dn_y, 1)
    hsend("h_xp", xh, yp, 1, over_x, 1)
    harrived("h_x", 1 - xh, y, 0, 1)
    hsend("h_gdn", 1 - xh, y, 0, dn_y, 1)
    hsend("h_gup", 1 - xh, y, 0, up_y, 1)
    harrived("h_up", xh, ym, 1, 1)
    hsend("h_xm", xh, ym, 1, over_x, 1)
    harrived("h_dn", xh, yp, 1, 0)
    hsend("h_xp", xh, yp, 1, over_x, 0)
    loads[2].wait()
    loads[3].wait()
    garrived("g_other", xl, z, 1 - c)
    garrived("g_xother", 1 - xl, z, 1 - c, 0)
    garrived("g_xother", 1 - xl, z, 1 - c, 1)
    project(z)
    garrived("g_xup", 1 - xl, zm, c, 0)
    gsend("g_xup2", 1 - xl, zm, c, up_z, 0)
    garrived("g_xdn", 1 - xl, zp, c, 1)
    gsend("g_xdn2", 1 - xl, zp, c, dn_z, 1)
    garrived("g_xup", 1 - xl, zm, c, 1)
    gsend("g_xupo", 1 - xl, zm, c, other)
    garrived("g_xdn", 1 - xl, zp, c, 0)
    gsend("g_xdno", 1 - xl, zp, c, other)
    garrived("g_upo", xl, zm, 1 - c)
    garrived("g_xupo", 1 - xl, zm, 1 - c)
    project(zm)
    harrived("h_gup", 1 - xh, ym, 0, 0)
    hsend("h_gup2", 1 - xh, ym, 0, up_y, 0)
    harrived("h_up2", xh, yf, 1, 0)
    hsend("h_xf", xh, yf, 1, over_x, 0)
    harrived("h_dn2", xh, yf, 1, 1)
    hsend("h_xf", xh, yf, 1, over_x, 1)
    harrived("h_gdn", 1 - xh, yp, 0, 1)
    hsend("h_gdn2", 1 - xh, yp, 0, dn_y, 1)
    release(0)
    release(1)
    garrived("g_up2", xl, zf, c, 0)
    garrived("g_dn2", xl, zf, c, 1)
    gsend("g_faro", xl, zf, c, other)
    garrived("g_dno", xl, zp, 1 - c)
    garrived("g_xdno", 1 - xl, zp, 1 - c)
    project(zp)
    release(2)
    garrived("g_xup2", 1 - xl, zf, c, 0)
    garrived("g_xdn2", 1 - xl, zf, c, 1)
    gsend("g_xfaro", 1 - xl, zf, c, other)
    garrived("g_faro", xl, zf, 1 - c)
    garrived("g_xfaro", 1 - xl, zf, 1 - c)
    project(zf)
    release(3)

    def add(at, p, ref):
        acc[at, rcols[p]] = (acc[at, rcols[p]].astype(F32) + ref[...].astype(F32)).astype(BF16)

    def meet(s):
        for d, (name, b) in enumerate((("p_far_up", yp), ("p_far_dn", ym))):
            arrived((name, s), pfar.at[s, d])
            add(rows(sides[s], b, d), 0, pfar.at[s, d])
            pnear_to(s, d, d)

    stores = []
    deep = features // 8

    def outer(f):
        at = pl.ds(f * deep, deep)
        gw[at, :] = lax.dot_general(
            go[:, at], hid[...], (((0,), (0,)), ((), ())), preferred_element_type=F32
        ).astype(BF16)
        store = pltpu.make_async_copy(gw.at[at], gw_out.at[at], local.at[4 + f])
        store.start()
        stores.append(store)

    def qadd(i):
        arrived(("q_x", i), qx.at[i])
        add(rows(xh, order[i]), 1, qx.at[i])

    def qfar_to(d):
        name, device = (("q_far_up", up_y), ("q_far_dn", dn_y))[d]
        send((name, 0), acc.at[rows(xh, yf, d), rcols[1]], qfar.at[d], device)

    def qnear_to(d, h):
        name, b, device = (("q_up", yp, up_y), ("q_dn", ym, dn_y))[d]
        send((name, h), acc.at[rows(xh, b, h), rcols[1]], qnear.at[d, pl.ds(h * half, half)], device)

    for h in (0, 1):
        harrived("h_x", 1 - xh, y, 1, h)
        harrived("h_xm", 1 - xh, ym, 1, h)
        harrived("h_xp", 1 - xh, yp, 1, h)
        harrived("h_xf", 1 - xh, yf, 1, h)
    harrived("h_up", xh, ym, 0, 1)
    harrived("h_dn", xh, yp, 0, 0)
    harrived("h_up2", xh, yf, 0, 0)
    harrived("h_dn2", xh, yf, 0, 1)
    harrived("h_gup", 1 - xh, ym, 0, 1)
    harrived("h_gdn", 1 - xh, yp, 0, 0)
    harrived("h_gup2", 1 - xh, yf, 0, 0)
    harrived("h_gdn2", 1 - xh, yf, 0, 1)
    for f in range(4):
        outer(f)
    qadd(0)
    outer(4)
    qadd(1)
    meet(0)
    outer(5)
    meet(1)
    qadd(2)
    outer(6)
    drain()

    def near_sum(s):
        for h in (0, 1):
            arrived(("p_up", s, h), pnear.at[s, 0, pl.ds(h * half, half)])
            arrived(("p_dn", s, h), pnear.at[s, 1, pl.ds(h * half, half)])

    near_sum(0)
    for h in (0, 1):
        at, piece = rows(1 - xh, y, h), pl.ds(h * half, half)
        total = acc[at, rcols[0]].astype(F32) + pnear[0, 0, piece].astype(F32) + pnear[0, 1, piece].astype(F32)
        acc[at, rcols[0]] = total.astype(BF16)
        send(("p_x", h), acc.at[at, rcols[0]], px.at[piece], over_x)
    qadd(3)
    for d in (0, 1):
        qfar_to(d)
    qnear_to(0, 1)
    qnear_to(1, 0)
    outer(7)
    for d, (name, b) in enumerate((("q_far_up", yp), ("q_far_dn", ym))):
        arrived((name, 0), qfar.at[d])
        add(rows(xh, b, d), 1, qfar.at[d])
        qnear_to(d, d)

    def finish(p, piece, total):
        gu[piece, rcols[p]] = (total * silu[piece, rcols[p]]).astype(BF16)
        gg[piece, rcols[p]] = (total * slope[piece, rcols[p]]).astype(BF16)

    near_sum(1)
    for h in (0, 1):
        piece = pl.ds(h * half, half)
        arrived(("p_x", h), px.at[piece])
        total = acc[rows(xh, y, h), rcols[0]].astype(F32) + px[piece].astype(F32)
        total = total + pnear[1, 0, piece].astype(F32) + pnear[1, 1, piece].astype(F32)
        finish(0, piece, total)
    for h in (0, 1):
        piece = pl.ds(h * half, half)
        arrived(("q_up", h), qnear.at[0, piece])
        arrived(("q_dn", h), qnear.at[1, piece])
        total = acc[rows(xh, y, h), rcols[1]].astype(F32)
        total = total + qnear[0, piece].astype(F32) + qnear[1, piece].astype(F32)
        finish(1, piece, total)
    stores.append(pltpu.make_async_copy(gg, gg_out, local.at[12]))
    stores.append(pltpu.make_async_copy(gu, gu_out, local.at[13]))
    stores[-1].start()
    stores[-2].start()
    for s in (0, 1):
        sent["p_far_up", s], sent["p_far_dn", s] = pfar.at[s, 0], pfar.at[s, 1]
        for h in (0, 1):
            sent["p_up", s, h] = sent["p_dn", s, h] = pnear.at[s, 0, pl.ds(h * half, half)]
    drain()
    for store in stores:
        store.wait()


def emit(gg_in, gu_in, gw_in, gg_out, gu_out, gw_out, sems):
    pieces = 8
    deep = gw_in.shape[0] // pieces
    copies = [pltpu.make_async_copy(gg_in, gg_out, sems.at[pieces]), pltpu.make_async_copy(gu_in, gu_out, sems.at[pieces + 1])]
    for i in range(pieces):
        at = pl.ds(i * deep, deep)
        copies.append(pltpu.make_async_copy(gw_in.at[at], gw_out.at[at], sems.at[i]))
    for copy in copies:
        copy.start()
    for copy in copies:
        copy.wait()


def on_device(grad_out, gate, up, w_down):
    own, units = gate.shape
    features = w_down.shape[0]
    tokens = own * NX * NY
    hsplit, split = 1024, 1024
    rest = units - split
    half = own // 2
    anywhere = pl.BlockSpec(memory_space=pl.ANY)
    results = pl.pallas_call(
        functools.partial(kernel, hsplit, split),
        out_shape=(
            jax.ShapeDtypeStruct((own, units), BF16),
            jax.ShapeDtypeStruct((own, units), BF16),
            jax.ShapeDtypeStruct((features, units), BF16),
        ),
        in_specs=[anywhere] * 4,
        out_specs=(anywhere,) * 3,
        scratch_shapes=[
            pltpu.VMEM((tokens, features), BF16),
            pltpu.VMEM((features, units), BF16),
            pltpu.VMEM((tokens, units), BF16),
            pltpu.VMEM((tokens, units), BF16),
            pltpu.VMEM((own, units), BF16),
            pltpu.VMEM((own, units), BF16),
            pltpu.VMEM((own, units), F32),
            pltpu.VMEM((own, units), F32),
            pltpu.VMEM((features, units), BF16),
            pltpu.VMEM((own, units), BF16),
            pltpu.VMEM((own, units), BF16),
            pltpu.VMEM((2, 2, half, split), BF16),
            pltpu.VMEM((2, 2, own, split), BF16),
            pltpu.VMEM((own, split), BF16),
            pltpu.VMEM((NY, own, rest), BF16),
            pltpu.VMEM((2, half, rest), BF16),
            pltpu.VMEM((2, own, rest), BF16),
            pltpu.SemaphoreType.DMA((14,)),
            pltpu.SemaphoreType.DMA((COPIES,)),
            pltpu.SemaphoreType.DMA((COPIES,)),
        ],
        compiler_params=pltpu.CompilerParams(
            collective_id=0, has_side_effects=True, vmem_limit_bytes=40 * 2**20
        ),
        cost_estimate=pl.CostEstimate(
            flops=4 * tokens * features * units, bytes_accessed=4 * features * units, transcendentals=own * units
        ),
    )(*[pltpu.with_memory_space_constraint(a, pltpu.HBM) for a in (grad_out, gate, up, w_down)])
    return pl.pallas_call(
        emit,
        out_shape=tuple(jax.ShapeDtypeStruct(r.shape, r.dtype) for r in results),
        in_specs=[pl.BlockSpec(memory_space=pl.ANY)] * 3,
        out_specs=(pl.BlockSpec(memory_space=pltpu.HBM),) * 3,
        scratch_shapes=[pltpu.SemaphoreType.DMA((10,))],
        compiler_params=pltpu.CompilerParams(vmem_limit_bytes=4 * 2**20),
    )(*[pltpu.with_memory_space_constraint(r, pltpu.VMEM) for r in results])


def solution(mesh):
    return jax.shard_map(
        on_device,
        mesh=mesh,
        in_specs=(P("col", "row"), P("row", "col"), P("row", "col"), P("row", "col")),
        out_specs=(P("row", "col"),) * 3,
        check_vma=False,
    )
```

```python
import functools

import jax
import jax.numpy as jnp
from jax import lax
from jax.experimental import pallas as pl
from jax.experimental.pallas import tpu as pltpu
from jax.sharding import PartitionSpec as P

MESH = pl.DeviceIdType.MESH
BF16, F32 = jnp.bfloat16, jnp.float32
NY, NX = 4, 2
COPIES = 96


def kernel(
    hsplit, rsplit, go_in, gate_in, up_in, w_in, gg, gu, gw,
    go, w, acc, hid, gate, up, silu, slope,
    pfar, pnear, px, qx, qfar, qnear, local, ssem, rsem,
):
    tokens, units = hid.shape
    features = go.shape[1]
    own = tokens // (NX * NY)
    half, part = own // 2, own // 2
    group = NX * own
    row, col = lax.axis_index("row"), lax.axis_index("col")
    xh, y = row // NY, row % NY
    xl, z, c = col // (2 * NY), (col // 2) % NY, col % 2
    yp, ym, yf = (y + 1) % NY, (y + 3) % NY, (y + 2) % NY
    zp, zm, zf = (z + 1) % NY, (z + 3) % NY, (z + 2) % NY
    up_y, dn_y, over_x = (xh * NY + yp, col), (xh * NY + ym, col), ((1 - xh) * NY + y, col)

    def at_col(a, b, d):
        return (row, a * (2 * NY) + b * 2 + d)

    up_z, dn_z = at_col(xl, zp, c), at_col(xl, zm, c)
    next_x, other = at_col(1 - xl, z, c), at_col(xl, z, 1 - c)
    peers = (up_y, dn_y, over_x, up_z, dn_z, next_x, other)

    hcols = (pl.ds(0, hsplit), pl.ds(hsplit, units - hsplit))
    rcols = (pl.ds(0, rsplit), pl.ds(rsplit, units - rsplit))

    def rows(a, b, h=None):
        start = b * group + a * own
        if h is None:
            return pl.ds(pl.multiple_of(start, own), own)
        return pl.ds(pl.multiple_of(start + h * half, half), half)

    def panel(a, b, d, h=None):
        start = b * group + a * own + d * part
        if h is None:
            return pl.ds(pl.multiple_of(start, part), part)
        return pl.ds(pl.multiple_of(start + h * (part // 2), part // 2), part // 2)

    names, sent = {}, {}

    def index(name):
        return names.setdefault(name, len(names))

    def send(name, src, dst, device, note=True):
        k = index(name)
        if note:
            sent[name] = dst
        pltpu.make_async_remote_copy(src, dst, ssem.at[k], rsem.at[k], device_id=device, device_id_type=MESH).start()

    def drain():
        for name, ref in sent.items():
            k = index(name)
            pltpu.make_async_remote_copy(ref, ref, ssem.at[k], rsem.at[k], device_id=other, device_id_type=MESH).wait_send()
        sent.clear()

    def arrived(name, dst):
        k = index(name)
        pltpu.make_async_remote_copy(dst, dst, ssem.at[k], rsem.at[k], device_id=other, device_id_type=MESH).wait_recv()

    loads = [
        pltpu.make_async_copy(gate_in, gate, local.at[0]),
        pltpu.make_async_copy(up_in, up, local.at[1]),
        pltpu.make_async_copy(go_in, go.at[panel(xl, z, c)], local.at[2]),
        pltpu.make_async_copy(w_in, w, local.at[3]),
    ]
    barrier = pltpu.get_barrier_semaphore()
    for peer in peers:
        pl.semaphore_signal(barrier, inc=1, device_id=peer, device_id_type=MESH)
    for load in loads[:3]:
        load.start()

    def gsend(name, a, b, d, device, h=None, src=None):
        ref = go.at[panel(a, b, d, h)]
        send((name, h), ref if src is None else src, ref, device)

    def garrived(name, a, b, d, h=None):
        arrived((name, h), go.at[panel(a, b, d, h)])

    def hsend(name, a, b, p, device, h):
        ref = hid.at[rows(a, b, h), hcols[p]]
        send((name, p, h), ref, ref, device)

    def harrived(name, a, b, p, h):
        arrived((name, p, h), hid.at[rows(a, b, h), hcols[p]])

    def activate(p, h):
        step = 16

        @pl.loop(0, half // step)
        def _(i):
            at = pl.ds(pl.multiple_of(h * half + i * step, step), step)
            to = pl.ds(pl.multiple_of(y * group + xh * own + h * half + i * step, step), step)
            v, u = gate[at, hcols[p]].astype(F32), up[at, hcols[p]].astype(F32)
            s = jax.nn.sigmoid(v)
            act = v * s
            silu[at, hcols[p]] = act
            slope[at, hcols[p]] = u * s * (1.0 + v * (1.0 - s))
            hid[to, hcols[p]] = (act * u).astype(BF16)

    pl.semaphore_wait(barrier, len(peers))
    pieces = [go_in.at[pl.ds(h * (part // 2), part // 2)] for h in (0, 1)]
    for h in (0, 1):
        gsend("g_next", xl, z, c, next_x, h, pieces[h])
        gsend("g_up", xl, z, c, up_z, h, pieces[h])
        gsend("g_dn", xl, z, c, dn_z, 1 - h, pieces[1 - h])
    gsend("g_other", xl, z, c, other, src=go_in)
    loads[0].wait()
    loads[1].wait()
    loads[3].start()
    for p in (0, 1):
        activate(p, 0)
        hsend("h_up", xh, y, p, up_y, 0)
        hsend("h_x", xh, y, p, over_x, 0)
        activate(p, 1)
        hsend("h_dn", xh, y, p, dn_y, 1)
        hsend("h_x", xh, y, p, over_x, 1)
        hsend("h_up", xh, y, p, up_y, 1)
        hsend("h_dn", xh, y, p, dn_y, 0)

    def project(b):
        at = pl.ds(pl.multiple_of(b * group, group), group)
        wide = 256

        @pl.loop(0, units // wide)
        def _(j):
            to = pl.ds(pl.multiple_of(j * wide, wide), wide)
            acc[at, to] = jnp.dot(go[at, :], w[:, to], preferred_element_type=F32).astype(BF16)

        rest = units % wide
        if rest:
            to = pl.ds(units - rest, rest)
            acc[at, to] = jnp.dot(go[at, :], w[:, to], preferred_element_type=F32).astype(BF16)

    sides = (1 - xh, xh)
    order = (z, zm, zp, zf)

    def pfar_to(s, d):
        name, device = (("p_far_up", up_y), ("p_far_dn", dn_y))[d]
        send((name, s), acc.at[rows(sides[s], yf, d), rcols[0]], pfar.at[s, d], device, False)

    def pnear_to(s, d, h):
        name, b, device = (("p_up", yp, up_y), ("p_dn", ym, dn_y))[d]
        to = pnear.at[s, d, pl.ds(h * half, half)]
        send((name, s, h), acc.at[rows(sides[s], b, h), rcols[0]], to, device, False)

    def release(i):
        send(("q_x", i), acc.at[rows(1 - xh, order[i]), rcols[1]], qx.at[i], over_x)
        away = (order[i] - y + NY) % NY

        @pl.when(away == 2)
        def _():
            for s in (0, 1):
                pfar_to(s, 0)
                pfar_to(s, 1)

        @pl.when(away == 1)
        def _():
            for s in (0, 1):
                pnear_to(s, 0, 1)

        @pl.when(away == 3)
        def _():
            for s in (0, 1):
                pnear_to(s, 1, 0)

    for h in (0, 1):
        garrived("g_next", 1 - xl, z, c, h)
        gsend("g_xup", 1 - xl, z, c, up_z, h)
        gsend("g_xdn", 1 - xl, z, c, dn_z, h)
        gsend("g_xother", 1 - xl, z, c, other, h)
        if h == 0:
            harrived("h_up", xh, ym, 0, 0)
            hsend("h_up2", xh, ym, 0, up_y, 0)
            harrived("h_dn", xh, yp, 0, 1)
            hsend("h_dn2", xh, yp, 0, dn_y, 1)
    garrived("g_up", xl, zm, c, 0)
    gsend("g_up2", xl, zm, c, up_z, 0)
    garrived("g_dn", xl, zp, c, 1)
    gsend("g_dn2", xl, zp, c, dn_z, 1)
    garrived("g_up", xl, zm, c, 1)
    gsend("g_upo", xl, zm, c, other)
    garrived("g_dn", xl, zp, c, 0)
    gsend("g_dno", xl, zp, c, other)
    harrived("h_x", 1 - xh, y, 0, 0)
    hsend("h_gup", 1 - xh, y, 0, up_y, 0)
    hsend("h_gdn", 1 - xh, y, 0, dn_y, 0)
    harrived("h_up", xh, ym, 1, 0)
    hsend("h_up2", xh, ym, 1, up_y, 0)
    hsend("h_xm", xh, ym, 1, over_x, 0)
    harrived("h_dn", xh, yp, 1, 1)
    hsend("h_dn2", xh, yp, 1, dn_y, 1)
    hsend("h_xp", xh, yp, 1, over_x, 1)
    harrived("h_x", 1 - xh, y, 0, 1)
    hsend("h_gdn", 1 - xh, y, 0, dn_y, 1)
    hsend("h_gup", 1 - xh, y, 0, up_y, 1)
    harrived("h_up", xh, ym, 1, 1)
    hsend("h_xm", xh, ym, 1, over_x, 1)
    harrived("h_dn", xh, yp, 1, 0)
    hsend("h_xp", xh, yp, 1, over_x, 0)
    loads[2].wait()
    loads[3].wait()
    garrived("g_other", xl, z, 1 - c)
    garrived("g_xother", 1 - xl, z, 1 - c, 0)
    garrived("g_xother", 1 - xl, z, 1 - c, 1)
    project(z)
    garrived("g_xup", 1 - xl, zm, c, 0)
    gsend("g_xup2", 1 - xl, zm, c, up_z, 0)
    garrived("g_xdn", 1 - xl, zp, c, 1)
    gsend("g_xdn2", 1 - xl, zp, c, dn_z, 1)
    garrived("g_xup", 1 - xl, zm, c, 1)
    gsend("g_xupo", 1 - xl, zm, c, other)
    garrived("g_xdn", 1 - xl, zp, c, 0)
    gsend("g_xdno", 1 - xl, zp, c, other)
    garrived("g_upo", xl, zm, 1 - c)
    garrived("g_xupo", 1 - xl, zm, 1 - c)
    project(zm)
    harrived("h_gup", 1 - xh, ym, 0, 0)
    hsend("h_gup2", 1 - xh, ym, 0, up_y, 0)
    harrived("h_up2", xh, yf, 1, 0)
    hsend("h_xf", xh, yf, 1, over_x, 0)
    harrived("h_dn2", xh, yf, 1, 1)
    hsend("h_xf", xh, yf, 1, over_x, 1)
    harrived("h_gdn", 1 - xh, yp, 0, 1)
    hsend("h_gdn2", 1 - xh, yp, 0, dn_y, 1)
    release(0)
    release(1)
    garrived("g_up2", xl, zf, c, 0)
    garrived("g_dn2", xl, zf, c, 1)
    gsend("g_faro", xl, zf, c, other)
    garrived("g_dno", xl, zp, 1 - c)
    garrived("g_xdno", 1 - xl, zp, 1 - c)
    project(zp)
    release(2)
    garrived("g_xup2", 1 - xl, zf, c, 0)
    garrived("g_xdn2", 1 - xl, zf, c, 1)
    gsend("g_xfaro", 1 - xl, zf, c, other)
    garrived("g_faro", xl, zf, 1 - c)
    garrived("g_xfaro", 1 - xl, zf, 1 - c)
    project(zf)
    release(3)

    def add(at, p, ref):
        acc[at, rcols[p]] = (acc[at, rcols[p]].astype(F32) + ref[...].astype(F32)).astype(BF16)

    def meet(s):
        for d, (name, b) in enumerate((("p_far_up", yp), ("p_far_dn", ym))):
            arrived((name, s), pfar.at[s, d])
            add(rows(sides[s], b, d), 0, pfar.at[s, d])
            pnear_to(s, d, d)

    deep = features // 8

    def outer(f):
        at = pl.ds(f * deep, deep)
        gw[at, :] = lax.dot_general(
            go[:, at], hid[...], (((0,), (0,)), ((), ())), preferred_element_type=F32
        ).astype(BF16)

    def qadd(i):
        arrived(("q_x", i), qx.at[i])
        add(rows(xh, order[i]), 1, qx.at[i])

    def qfar_to(d):
        name, device = (("q_far_up", up_y), ("q_far_dn", dn_y))[d]
        send((name, 0), acc.at[rows(xh, yf, d), rcols[1]], qfar.at[d], device)

    def qnear_to(d, h):
        name, b, device = (("q_up", yp, up_y), ("q_dn", ym, dn_y))[d]
        send((name, h), acc.at[rows(xh, b, h), rcols[1]], qnear.at[d, pl.ds(h * half, half)], device)

    for h in (0, 1):
        harrived("h_x", 1 - xh, y, 1, h)
        harrived("h_xm", 1 - xh, ym, 1, h)
        harrived("h_xp", 1 - xh, yp, 1, h)
        harrived("h_xf", 1 - xh, yf, 1, h)
    harrived("h_up", xh, ym, 0, 1)
    harrived("h_dn", xh, yp, 0, 0)
    harrived("h_up2", xh, yf, 0, 0)
    harrived("h_dn2", xh, yf, 0, 1)
    harrived("h_gup", 1 - xh, ym, 0, 1)
    harrived("h_gdn", 1 - xh, yp, 0, 0)
    harrived("h_gup2", 1 - xh, yf, 0, 0)
    harrived("h_gdn2", 1 - xh, yf, 0, 1)
    def near_sum(s):
        for h in (0, 1):
            arrived(("p_up", s, h), pnear.at[s, 0, pl.ds(h * half, half)])
            arrived(("p_dn", s, h), pnear.at[s, 1, pl.ds(h * half, half)])

    outer(0)
    outer(1)
    outer(2)
    outer(3)
    meet(0)
    qadd(0)
    outer(4)
    qadd(1)
    meet(1)
    outer(5)
    qadd(2)
    outer(6)
    drain()
    near_sum(0)
    for h in (0, 1):
        at, piece = rows(1 - xh, y, h), pl.ds(h * half, half)
        total = acc[at, rcols[0]].astype(F32) + pnear[0, 0, piece].astype(F32) + pnear[0, 1, piece].astype(F32)
        acc[at, rcols[0]] = total.astype(BF16)
        send(("p_x", h), acc.at[at, rcols[0]], px.at[piece], over_x)
    qadd(3)
    for d in (0, 1):
        qfar_to(d)
    qnear_to(0, 1)
    qnear_to(1, 0)
    outer(7)
    for d, (name, b) in enumerate((("q_far_up", yp), ("q_far_dn", ym))):
        arrived((name, 0), qfar.at[d])
        add(rows(xh, b, d), 1, qfar.at[d])
        qnear_to(d, d)

    def finish(p, piece, total):
        gu[piece, rcols[p]] = (total * silu[piece, rcols[p]]).astype(BF16)
        gg[piece, rcols[p]] = (total * slope[piece, rcols[p]]).astype(BF16)

    near_sum(1)
    for h in (0, 1):
        piece = pl.ds(h * half, half)
        arrived(("p_x", h), px.at[piece])
        total = acc[rows(xh, y, h), rcols[0]].astype(F32) + px[piece].astype(F32)
        total = total + pnear[1, 0, piece].astype(F32) + pnear[1, 1, piece].astype(F32)
        finish(0, piece, total)
    for h in (0, 1):
        piece = pl.ds(h * half, half)
        arrived(("q_up", h), qnear.at[0, piece])
        arrived(("q_dn", h), qnear.at[1, piece])
        total = acc[rows(xh, y, h), rcols[1]].astype(F32)
        total = total + qnear[0, piece].astype(F32) + qnear[1, piece].astype(F32)
        finish(1, piece, total)
    for s in (0, 1):
        sent["p_far_up", s], sent["p_far_dn", s] = pfar.at[s, 0], pfar.at[s, 1]
        for h in (0, 1):
            sent["p_up", s, h] = sent["p_dn", s, h] = pnear.at[s, 0, pl.ds(h * half, half)]
    drain()


def emit(gg_in, gu_in, gw_in, gg_out, gu_out, gw_out, sems):
    pieces = 8
    deep = gw_in.shape[0] // pieces
    copies = [pltpu.make_async_copy(gg_in, gg_out, sems.at[pieces]), pltpu.make_async_copy(gu_in, gu_out, sems.at[pieces + 1])]
    for i in range(pieces):
        at = pl.ds(i * deep, deep)
        copies.append(pltpu.make_async_copy(gw_in.at[at], gw_out.at[at], sems.at[i]))
    for copy in copies:
        copy.start()
    for copy in copies:
        copy.wait()


def on_device(grad_out, gate, up, w_down):
    own, units = gate.shape
    features = w_down.shape[0]
    tokens = own * NX * NY
    hsplit, split = 1024, 1024
    rest = units - split
    half = own // 2
    anywhere = pl.BlockSpec(memory_space=pl.ANY)
    results = pl.pallas_call(
        functools.partial(kernel, hsplit, split),
        out_shape=(
            jax.ShapeDtypeStruct((own, units), BF16),
            jax.ShapeDtypeStruct((own, units), BF16),
            jax.ShapeDtypeStruct((features, units), BF16),
        ),
        in_specs=[anywhere] * 4,
        out_specs=(pl.BlockSpec(memory_space=pltpu.VMEM),) * 3,
        scratch_shapes=[
            pltpu.VMEM((tokens, features), BF16),
            pltpu.VMEM((features, units), BF16),
            pltpu.VMEM((tokens, units), BF16),
            pltpu.VMEM((tokens, units), BF16),
            pltpu.VMEM((own, units), BF16),
            pltpu.VMEM((own, units), BF16),
            pltpu.VMEM((own, units), F32),
            pltpu.VMEM((own, units), F32),
            pltpu.VMEM((2, 2, half, split), BF16),
            pltpu.VMEM((2, 2, own, split), BF16),
            pltpu.VMEM((own, split), BF16),
            pltpu.VMEM((NY, own, rest), BF16),
            pltpu.VMEM((2, half, rest), BF16),
            pltpu.VMEM((2, own, rest), BF16),
            pltpu.SemaphoreType.DMA((4,)),
            pltpu.SemaphoreType.DMA((COPIES,)),
            pltpu.SemaphoreType.DMA((COPIES,)),
        ],
        compiler_params=pltpu.CompilerParams(
            collective_id=0, has_side_effects=True, vmem_limit_bytes=40 * 2**20
        ),
        cost_estimate=pl.CostEstimate(
            flops=4 * tokens * features * units, bytes_accessed=4 * features * units, transcendentals=own * units
        ),
    )(*[pltpu.with_memory_space_constraint(a, pltpu.HBM) for a in (grad_out, gate, up, w_down)])
    return pl.pallas_call(
        emit,
        out_shape=tuple(jax.ShapeDtypeStruct(r.shape, r.dtype) for r in results),
        in_specs=[pl.BlockSpec(memory_space=pl.ANY)] * 3,
        out_specs=(pl.BlockSpec(memory_space=pltpu.HBM),) * 3,
        scratch_shapes=[pltpu.SemaphoreType.DMA((10,))],
        compiler_params=pltpu.CompilerParams(vmem_limit_bytes=4 * 2**20),
    )(*[pltpu.with_memory_space_constraint(r, pltpu.VMEM) for r in results])


def solution(mesh):
    return jax.shard_map(
        on_device,
        mesh=mesh,
        in_specs=(P("col", "row"), P("row", "col"), P("row", "col"), P("row", "col")),
        out_specs=(P("row", "col"),) * 3,
        check_vma=False,
    )
```

```python
import functools

import jax
import jax.numpy as jnp
from jax import lax
from jax.experimental import pallas as pl
from jax.experimental.pallas import tpu as pltpu
from jax.sharding import PartitionSpec as P

MESH = pl.DeviceIdType.MESH
BF16, F32 = jnp.bfloat16, jnp.float32
NY, NX = 4, 2
COPIES = 96


def kernel(
    hsplit, rsplit, go_in, gate_in, up_in, w_in, gg, gu, gw,
    go, w, acc, hid, gate, up, silu, slope,
    pfar, pnear, px, qx, qfar, qnear, local, ssem, rsem,
):
    tokens, units = hid.shape
    features = go.shape[1]
    own = tokens // (NX * NY)
    half, part = own // 2, own // 2
    group = NX * own
    row, col = lax.axis_index("row"), lax.axis_index("col")
    xh, y = row // NY, row % NY
    xl, z, c = col // (2 * NY), (col // 2) % NY, col % 2
    yp, ym, yf = (y + 1) % NY, (y + 3) % NY, (y + 2) % NY
    zp, zm, zf = (z + 1) % NY, (z + 3) % NY, (z + 2) % NY
    up_y, dn_y, over_x = (xh * NY + yp, col), (xh * NY + ym, col), ((1 - xh) * NY + y, col)

    def at_col(a, b, d):
        return (row, a * (2 * NY) + b * 2 + d)

    up_z, dn_z = at_col(xl, zp, c), at_col(xl, zm, c)
    next_x, other = at_col(1 - xl, z, c), at_col(xl, z, 1 - c)
    peers = (up_y, dn_y, over_x, up_z, dn_z, next_x, other)

    hcols = (pl.ds(0, hsplit), pl.ds(hsplit, units - hsplit))
    rcols = (pl.ds(0, rsplit), pl.ds(rsplit, units - rsplit))

    def rows(a, b, h=None):
        start = b * group + a * own
        if h is None:
            return pl.ds(pl.multiple_of(start, own), own)
        return pl.ds(pl.multiple_of(start + h * half, half), half)

    def panel(a, b, d, h=None):
        start = b * group + a * own + d * part
        if h is None:
            return pl.ds(pl.multiple_of(start, part), part)
        return pl.ds(pl.multiple_of(start + h * (part // 2), part // 2), part // 2)

    names, sent = {}, {}

    def index(name):
        return names.setdefault(name, len(names))

    def send(name, src, dst, device, note=True):
        k = index(name)
        if note:
            sent[name] = dst
        pltpu.make_async_remote_copy(src, dst, ssem.at[k], rsem.at[k], device_id=device, device_id_type=MESH).start()

    def drain():
        for name, ref in sent.items():
            k = index(name)
            pltpu.make_async_remote_copy(ref, ref, ssem.at[k], rsem.at[k], device_id=other, device_id_type=MESH).wait_send()
        sent.clear()

    def arrived(name, dst):
        k = index(name)
        pltpu.make_async_remote_copy(dst, dst, ssem.at[k], rsem.at[k], device_id=other, device_id_type=MESH).wait_recv()

    loads = [
        pltpu.make_async_copy(gate_in.at[:, hcols[0]], gate.at[:, hcols[0]], local.at[0]),
        pltpu.make_async_copy(up_in.at[:, hcols[0]], up.at[:, hcols[0]], local.at[1]),
        pltpu.make_async_copy(gate_in.at[:, hcols[1]], gate.at[:, hcols[1]], local.at[2]),
        pltpu.make_async_copy(up_in.at[:, hcols[1]], up.at[:, hcols[1]], local.at[3]),
        pltpu.make_async_copy(go_in, go.at[panel(xl, z, c)], local.at[4]),
        pltpu.make_async_copy(w_in, w, local.at[5]),
    ]
    barrier = pltpu.get_barrier_semaphore()
    for peer in peers:
        pl.semaphore_signal(barrier, inc=1, device_id=peer, device_id_type=MESH)
    for load in loads[:5]:
        load.start()

    def gsend(name, a, b, d, device, h=None, src=None):
        ref = go.at[panel(a, b, d, h)]
        send((name, h), ref if src is None else src, ref, device)

    def garrived(name, a, b, d, h=None):
        arrived((name, h), go.at[panel(a, b, d, h)])

    def hsend(name, a, b, p, device, h):
        ref = hid.at[rows(a, b, h), hcols[p]]
        send((name, p, h), ref, ref, device)

    def harrived(name, a, b, p, h):
        arrived((name, p, h), hid.at[rows(a, b, h), hcols[p]])

    def activate(p, h):
        step = 16

        @pl.loop(0, half // step)
        def _(i):
            at = pl.ds(pl.multiple_of(h * half + i * step, step), step)
            to = pl.ds(pl.multiple_of(y * group + xh * own + h * half + i * step, step), step)
            v, u = gate[at, hcols[p]].astype(F32), up[at, hcols[p]].astype(F32)
            s = jax.nn.sigmoid(v)
            act = v * s
            silu[at, hcols[p]] = act
            slope[at, hcols[p]] = u * s * (1.0 + v * (1.0 - s))
            hid[to, hcols[p]] = (act * u).astype(BF16)

    pl.semaphore_wait(barrier, len(peers))
    pieces = [go_in.at[pl.ds(h * (part // 2), part // 2)] for h in (0, 1)]
    for h in (0, 1):
        gsend("g_next", xl, z, c, next_x, h, pieces[h])
        gsend("g_up", xl, z, c, up_z, h, pieces[h])
        gsend("g_dn", xl, z, c, dn_z, 1 - h, pieces[1 - h])
    gsend("g_other", xl, z, c, other, src=go_in)
    for p in (0, 1):
        loads[2 * p].wait()
        loads[2 * p + 1].wait()
        if p == 1:
            loads[5].start()
        activate(p, 0)
        hsend("h_up", xh, y, p, up_y, 0)
        hsend("h_x", xh, y, p, over_x, 0)
        activate(p, 1)
        hsend("h_dn", xh, y, p, dn_y, 1)
        hsend("h_x", xh, y, p, over_x, 1)
        hsend("h_up", xh, y, p, up_y, 1)
        hsend("h_dn", xh, y, p, dn_y, 0)

    def project(b):
        at = pl.ds(pl.multiple_of(b * group, group), group)
        wide = 256

        @pl.loop(0, units // wide)
        def _(j):
            to = pl.ds(pl.multiple_of(j * wide, wide), wide)
            acc[at, to] = jnp.dot(go[at, :], w[:, to], preferred_element_type=F32).astype(BF16)

        rest = units % wide
        if rest:
            to = pl.ds(units - rest, rest)
            acc[at, to] = jnp.dot(go[at, :], w[:, to], preferred_element_type=F32).astype(BF16)

    sides = (1 - xh, xh)
    order = (z, zm, zp, zf)

    def pfar_to(s, d):
        name, device = (("p_far_up", up_y), ("p_far_dn", dn_y))[d]
        send((name, s), acc.at[rows(sides[s], yf, d), rcols[0]], pfar.at[s, d], device, False)

    def pnear_to(s, d, h):
        name, b, device = (("p_up", yp, up_y), ("p_dn", ym, dn_y))[d]
        to = pnear.at[s, d, pl.ds(h * half, half)]
        send((name, s, h), acc.at[rows(sides[s], b, h), rcols[0]], to, device, False)

    def release(i):
        send(("q_x", i), acc.at[rows(1 - xh, order[i]), rcols[1]], qx.at[i], over_x)
        away = (order[i] - y + NY) % NY

        @pl.when(away == 2)
        def _():
            for s in (0, 1):
                pfar_to(s, 0)
                pfar_to(s, 1)

        @pl.when(away == 1)
        def _():
            for s in (0, 1):
                pnear_to(s, 0, 1)

        @pl.when(away == 3)
        def _():
            for s in (0, 1):
                pnear_to(s, 1, 0)

    for h in (0, 1):
        garrived("g_next", 1 - xl, z, c, h)
        gsend("g_xup", 1 - xl, z, c, up_z, h)
        gsend("g_xdn", 1 - xl, z, c, dn_z, h)
        gsend("g_xother", 1 - xl, z, c, other, h)
        if h == 0:
            harrived("h_up", xh, ym, 0, 0)
            hsend("h_up2", xh, ym, 0, up_y, 0)
            harrived("h_dn", xh, yp, 0, 1)
            hsend("h_dn2", xh, yp, 0, dn_y, 1)
    garrived("g_up", xl, zm, c, 0)
    gsend("g_up2", xl, zm, c, up_z, 0)
    garrived("g_dn", xl, zp, c, 1)
    gsend("g_dn2", xl, zp, c, dn_z, 1)
    garrived("g_up", xl, zm, c, 1)
    gsend("g_upo", xl, zm, c, other)
    garrived("g_dn", xl, zp, c, 0)
    gsend("g_dno", xl, zp, c, other)
    harrived("h_x", 1 - xh, y, 0, 0)
    hsend("h_gup", 1 - xh, y, 0, up_y, 0)
    hsend("h_gdn", 1 - xh, y, 0, dn_y, 0)
    harrived("h_up", xh, ym, 1, 0)
    hsend("h_up2", xh, ym, 1, up_y, 0)
    hsend("h_xm", xh, ym, 1, over_x, 0)
    harrived("h_dn", xh, yp, 1, 1)
    hsend("h_dn2", xh, yp, 1, dn_y, 1)
    hsend("h_xp", xh, yp, 1, over_x, 1)
    harrived("h_x", 1 - xh, y, 0, 1)
    hsend("h_gdn", 1 - xh, y, 0, dn_y, 1)
    hsend("h_gup", 1 - xh, y, 0, up_y, 1)
    harrived("h_up", xh, ym, 1, 1)
    hsend("h_xm", xh, ym, 1, over_x, 1)
    harrived("h_dn", xh, yp, 1, 0)
    hsend("h_xp", xh, yp, 1, over_x, 0)
    loads[4].wait()
    loads[5].wait()
    garrived("g_other", xl, z, 1 - c)
    garrived("g_xother", 1 - xl, z, 1 - c, 0)
    garrived("g_xother", 1 - xl, z, 1 - c, 1)
    project(z)
    garrived("g_xup", 1 - xl, zm, c, 0)
    gsend("g_xup2", 1 - xl, zm, c, up_z, 0)
    garrived("g_xdn", 1 - xl, zp, c, 1)
    gsend("g_xdn2", 1 - xl, zp, c, dn_z, 1)
    garrived("g_xup", 1 - xl, zm, c, 1)
    gsend("g_xupo", 1 - xl, zm, c, other)
    garrived("g_xdn", 1 - xl, zp, c, 0)
    gsend("g_xdno", 1 - xl, zp, c, other)
    garrived("g_upo", xl, zm, 1 - c)
    garrived("g_xupo", 1 - xl, zm, 1 - c)
    project(zm)
    harrived("h_gup", 1 - xh, ym, 0, 0)
    hsend("h_gup2", 1 - xh, ym, 0, up_y, 0)
    harrived("h_up2", xh, yf, 1, 0)
    hsend("h_xf", xh, yf, 1, over_x, 0)
    harrived("h_dn2", xh, yf, 1, 1)
    hsend("h_xf", xh, yf, 1, over_x, 1)
    harrived("h_gdn", 1 - xh, yp, 0, 1)
    hsend("h_gdn2", 1 - xh, yp, 0, dn_y, 1)
    release(0)
    release(1)
    garrived("g_up2", xl, zf, c, 0)
    garrived("g_dn2", xl, zf, c, 1)
    gsend("g_faro", xl, zf, c, other)
    garrived("g_dno", xl, zp, 1 - c)
    garrived("g_xdno", 1 - xl, zp, 1 - c)
    project(zp)
    release(2)
    garrived("g_xup2", 1 - xl, zf, c, 0)
    garrived("g_xdn2", 1 - xl, zf, c, 1)
    gsend("g_xfaro", 1 - xl, zf, c, other)
    garrived("g_faro", xl, zf, 1 - c)
    garrived("g_xfaro", 1 - xl, zf, 1 - c)
    project(zf)
    release(3)

    def add(at, p, ref):
        acc[at, rcols[p]] = (acc[at, rcols[p]].astype(F32) + ref[...].astype(F32)).astype(BF16)

    def meet(s):
        for d, (name, b) in enumerate((("p_far_up", yp), ("p_far_dn", ym))):
            arrived((name, s), pfar.at[s, d])
            add(rows(sides[s], b, d), 0, pfar.at[s, d])
            pnear_to(s, d, d)

    deep = features // 8

    def outer(f):
        at = pl.ds(f * deep, deep)
        gw[at, :] = lax.dot_general(
            go[:, at], hid[...], (((0,), (0,)), ((), ())), preferred_element_type=F32
        ).astype(BF16)

    def qadd(i):
        arrived(("q_x", i), qx.at[i])
        add(rows(xh, order[i]), 1, qx.at[i])

    def qfar_to(d):
        name, device = (("q_far_up", up_y), ("q_far_dn", dn_y))[d]
        send((name, 0), acc.at[rows(xh, yf, d), rcols[1]], qfar.at[d], device)

    def qnear_to(d, h):
        name, b, device = (("q_up", yp, up_y), ("q_dn", ym, dn_y))[d]
        send((name, h), acc.at[rows(xh, b, h), rcols[1]], qnear.at[d, pl.ds(h * half, half)], device)

    for h in (0, 1):
        harrived("h_x", 1 - xh, y, 1, h)
        harrived("h_xm", 1 - xh, ym, 1, h)
        harrived("h_xp", 1 - xh, yp, 1, h)
        harrived("h_xf", 1 - xh, yf, 1, h)
    harrived("h_up", xh, ym, 0, 1)
    harrived("h_dn", xh, yp, 0, 0)
    harrived("h_up2", xh, yf, 0, 0)
    harrived("h_dn2", xh, yf, 0, 1)
    harrived("h_gup", 1 - xh, ym, 0, 1)
    harrived("h_gdn", 1 - xh, yp, 0, 0)
    harrived("h_gup2", 1 - xh, yf, 0, 0)
    harrived("h_gdn2", 1 - xh, yf, 0, 1)
    def near_sum(s):
        for h in (0, 1):
            arrived(("p_up", s, h), pnear.at[s, 0, pl.ds(h * half, half)])
            arrived(("p_dn", s, h), pnear.at[s, 1, pl.ds(h * half, half)])

    outer(0)
    outer(1)
    outer(2)
    outer(3)
    meet(0)
    qadd(0)
    outer(4)
    qadd(1)
    meet(1)
    outer(5)
    qadd(2)
    outer(6)
    drain()
    for h in (0, 1):
        at, piece = rows(1 - xh, y, h), pl.ds(h * half, half)
        arrived(("p_up", 0, h), pnear.at[0, 0, piece])
        arrived(("p_dn", 0, h), pnear.at[0, 1, piece])
        total = acc[at, rcols[0]].astype(F32) + pnear[0, 0, piece].astype(F32) + pnear[0, 1, piece].astype(F32)
        acc[at, rcols[0]] = total.astype(BF16)
        send(("p_x", h), acc.at[at, rcols[0]], px.at[piece], over_x)
    qadd(3)
    for d in (0, 1):
        qfar_to(d)
    qnear_to(0, 1)
    qnear_to(1, 0)
    outer(7)
    for d, (name, b) in enumerate((("q_far_up", yp), ("q_far_dn", ym))):
        arrived((name, 0), qfar.at[d])
        add(rows(xh, b, d), 1, qfar.at[d])
        qnear_to(d, d)

    def finish(p, piece, total):
        gu[piece, rcols[p]] = (total * silu[piece, rcols[p]]).astype(BF16)
        gg[piece, rcols[p]] = (total * slope[piece, rcols[p]]).astype(BF16)

    near_sum(1)
    for h in (0, 1):
        piece = pl.ds(h * half, half)
        arrived(("p_x", h), px.at[piece])
        total = acc[rows(xh, y, h), rcols[0]].astype(F32) + px[piece].astype(F32)
        total = total + pnear[1, 0, piece].astype(F32) + pnear[1, 1, piece].astype(F32)
        finish(0, piece, total)
    for h in (0, 1):
        piece = pl.ds(h * half, half)
        arrived(("q_up", h), qnear.at[0, piece])
        arrived(("q_dn", h), qnear.at[1, piece])
        total = acc[rows(xh, y, h), rcols[1]].astype(F32)
        total = total + qnear[0, piece].astype(F32) + qnear[1, piece].astype(F32)
        finish(1, piece, total)
    for s in (0, 1):
        sent["p_far_up", s], sent["p_far_dn", s] = pfar.at[s, 0], pfar.at[s, 1]
        for h in (0, 1):
            sent["p_up", s, h] = sent["p_dn", s, h] = pnear.at[s, 0, pl.ds(h * half, half)]
    drain()


def emit(gg_in, gu_in, gw_in, gg_out, gu_out, gw_out, sems):
    pieces = 8
    deep = gw_in.shape[0] // pieces
    copies = [pltpu.make_async_copy(gg_in, gg_out, sems.at[pieces]), pltpu.make_async_copy(gu_in, gu_out, sems.at[pieces + 1])]
    for i in range(pieces):
        at = pl.ds(i * deep, deep)
        copies.append(pltpu.make_async_copy(gw_in.at[at], gw_out.at[at], sems.at[i]))
    for copy in copies:
        copy.start()
    for copy in copies:
        copy.wait()


def on_device(grad_out, gate, up, w_down):
    own, units = gate.shape
    features = w_down.shape[0]
    tokens = own * NX * NY
    hsplit, split = 1024, 1024
    rest = units - split
    half = own // 2
    anywhere = pl.BlockSpec(memory_space=pl.ANY)
    results = pl.pallas_call(
        functools.partial(kernel, hsplit, split),
        out_shape=(
            jax.ShapeDtypeStruct((own, units), BF16),
            jax.ShapeDtypeStruct((own, units), BF16),
            jax.ShapeDtypeStruct((features, units), BF16),
        ),
        in_specs=[anywhere] * 4,
        out_specs=(pl.BlockSpec(memory_space=pltpu.VMEM),) * 3,
        scratch_shapes=[
            pltpu.VMEM((tokens, features), BF16),
            pltpu.VMEM((features, units), BF16),
            pltpu.VMEM((tokens, units), BF16),
            pltpu.VMEM((tokens, units), BF16),
            pltpu.VMEM((own, units), BF16),
            pltpu.VMEM((own, units), BF16),
            pltpu.VMEM((own, units), F32),
            pltpu.VMEM((own, units), F32),
            pltpu.VMEM((2, 2, half, split), BF16),
            pltpu.VMEM((2, 2, own, split), BF16),
            pltpu.VMEM((own, split), BF16),
            pltpu.VMEM((NY, own, rest), BF16),
            pltpu.VMEM((2, half, rest), BF16),
            pltpu.VMEM((2, own, rest), BF16),
            pltpu.SemaphoreType.DMA((6,)),
            pltpu.SemaphoreType.DMA((COPIES,)),
            pltpu.SemaphoreType.DMA((COPIES,)),
        ],
        compiler_params=pltpu.CompilerParams(
            collective_id=0, has_side_effects=True, vmem_limit_bytes=40 * 2**20
        ),
        cost_estimate=pl.CostEstimate(
            flops=4 * tokens * features * units, bytes_accessed=4 * features * units, transcendentals=own * units
        ),
    )(*[pltpu.with_memory_space_constraint(a, pltpu.HBM) for a in (grad_out, gate, up, w_down)])
    return pl.pallas_call(
        emit,
        out_shape=tuple(jax.ShapeDtypeStruct(r.shape, r.dtype) for r in results),
        in_specs=[pl.BlockSpec(memory_space=pl.ANY)] * 3,
        out_specs=(pl.BlockSpec(memory_space=pltpu.HBM),) * 3,
        scratch_shapes=[pltpu.SemaphoreType.DMA((10,))],
        compiler_params=pltpu.CompilerParams(vmem_limit_bytes=4 * 2**20),
    )(*[pltpu.with_memory_space_constraint(r, pltpu.VMEM) for r in results])


def solution(mesh):
    return jax.shard_map(
        on_device,
        mesh=mesh,
        in_specs=(P("col", "row"), P("row", "col"), P("row", "col"), P("row", "col")),
        out_specs=(P("row", "col"),) * 3,
        check_vma=False,
    )
```

```python
import functools

import jax
import jax.numpy as jnp
from jax import lax
from jax.experimental import pallas as pl
from jax.experimental.pallas import tpu as pltpu
from jax.sharding import PartitionSpec as P

MESH = pl.DeviceIdType.MESH
BF16, F32 = jnp.bfloat16, jnp.float32
NY, NX = 4, 2
COPIES = 96


def kernel(
    hsplit, rsplit, go_in, gate_in, up_in, w_in, gg, gu, gw,
    go, w, acc, hid, gate, up, silu, slope,
    pfar, pnear, px, qx, qfar, qnear, local, ssem, rsem,
):
    tokens, units = hid.shape
    features = go.shape[1]
    own = tokens // (NX * NY)
    half, part = own // 2, own // 2
    group = NX * own
    row, col = lax.axis_index("row"), lax.axis_index("col")
    xh, y = row // NY, row % NY
    xl, z, c = col // (2 * NY), (col // 2) % NY, col % 2
    yp, ym, yf = (y + 1) % NY, (y + 3) % NY, (y + 2) % NY
    zp, zm, zf = (z + 1) % NY, (z + 3) % NY, (z + 2) % NY
    up_y, dn_y, over_x = (xh * NY + yp, col), (xh * NY + ym, col), ((1 - xh) * NY + y, col)

    def at_col(a, b, d):
        return (row, a * (2 * NY) + b * 2 + d)

    up_z, dn_z = at_col(xl, zp, c), at_col(xl, zm, c)
    next_x, other = at_col(1 - xl, z, c), at_col(xl, z, 1 - c)
    peers = (up_y, dn_y, over_x, up_z, dn_z, next_x, other)

    hcols = (pl.ds(0, hsplit), pl.ds(hsplit, units - hsplit))
    rcols = (pl.ds(0, rsplit), pl.ds(rsplit, units - rsplit))

    def rows(a, b, h=None):
        start = b * group + a * own
        if h is None:
            return pl.ds(pl.multiple_of(start, own), own)
        return pl.ds(pl.multiple_of(start + h * half, half), half)

    def panel(a, b, d, h=None):
        start = b * group + a * own + d * part
        if h is None:
            return pl.ds(pl.multiple_of(start, part), part)
        return pl.ds(pl.multiple_of(start + h * (part // 2), part // 2), part // 2)

    names, sent = {}, {}

    def index(name):
        return names.setdefault(name, len(names))

    def send(name, src, dst, device, note=True):
        k = index(name)
        if note:
            sent[name] = dst
        pltpu.make_async_remote_copy(src, dst, ssem.at[k], rsem.at[k], device_id=device, device_id_type=MESH).start()

    def drain():
        for name, ref in sent.items():
            k = index(name)
            pltpu.make_async_remote_copy(ref, ref, ssem.at[k], rsem.at[k], device_id=other, device_id_type=MESH).wait_send()
        sent.clear()

    def arrived(name, dst):
        k = index(name)
        pltpu.make_async_remote_copy(dst, dst, ssem.at[k], rsem.at[k], device_id=other, device_id_type=MESH).wait_recv()

    loads = [
        pltpu.make_async_copy(gate_in.at[:, hcols[0]], gate.at[:, hcols[0]], local.at[0]),
        pltpu.make_async_copy(up_in.at[:, hcols[0]], up.at[:, hcols[0]], local.at[1]),
        pltpu.make_async_copy(gate_in.at[:, hcols[1]], gate.at[:, hcols[1]], local.at[2]),
        pltpu.make_async_copy(up_in.at[:, hcols[1]], up.at[:, hcols[1]], local.at[3]),
        pltpu.make_async_copy(go_in, go.at[panel(xl, z, c)], local.at[4]),
        pltpu.make_async_copy(w_in, w, local.at[5]),
    ]
    barrier = pltpu.get_barrier_semaphore()
    for peer in peers:
        pl.semaphore_signal(barrier, inc=1, device_id=peer, device_id_type=MESH)
    for load in loads[:5]:
        load.start()

    def gsend(name, a, b, d, device, h=None, src=None):
        ref = go.at[panel(a, b, d, h)]
        send((name, h), ref if src is None else src, ref, device)

    def garrived(name, a, b, d, h=None):
        arrived((name, h), go.at[panel(a, b, d, h)])

    def hsend(name, a, b, p, device, h):
        ref = hid.at[rows(a, b, h), hcols[p]]
        send((name, p, h), ref, ref, device)

    def harrived(name, a, b, p, h):
        arrived((name, p, h), hid.at[rows(a, b, h), hcols[p]])

    def activate(p, h):
        step = 16

        @pl.loop(0, half // step)
        def _(i):
            at = pl.ds(pl.multiple_of(h * half + i * step, step), step)
            to = pl.ds(pl.multiple_of(y * group + xh * own + h * half + i * step, step), step)
            v, u = gate[at, hcols[p]].astype(F32), up[at, hcols[p]].astype(F32)
            s = jax.nn.sigmoid(v)
            act = v * s
            silu[at, hcols[p]] = act
            slope[at, hcols[p]] = u * s * (1.0 + v * (1.0 - s))
            hid[to, hcols[p]] = (act * u).astype(BF16)

    pl.semaphore_wait(barrier, len(peers))
    pieces = [go_in.at[pl.ds(h * (part // 2), part // 2)] for h in (0, 1)]
    for h in (0, 1):
        gsend("g_next", xl, z, c, next_x, h, pieces[h])
        gsend("g_up", xl, z, c, up_z, h, pieces[h])
        gsend("g_dn", xl, z, c, dn_z, 1 - h, pieces[1 - h])
    gsend("g_other", xl, z, c, other, src=go_in)
    for p in (0, 1):
        loads[2 * p].wait()
        loads[2 * p + 1].wait()
        if p == 1:
            loads[5].start()
        activate(p, 0)
        hsend("h_up", xh, y, p, up_y, 0)
        hsend("h_x", xh, y, p, over_x, 0)
        activate(p, 1)
        hsend("h_dn", xh, y, p, dn_y, 1)
        hsend("h_x", xh, y, p, over_x, 1)
        hsend("h_up", xh, y, p, up_y, 1)
        hsend("h_dn", xh, y, p, dn_y, 0)

    def project(b):
        at = pl.ds(pl.multiple_of(b * group, group), group)
        wide = 256

        @pl.loop(0, units // wide)
        def _(j):
            to = pl.ds(pl.multiple_of(j * wide, wide), wide)
            acc[at, to] = jnp.dot(go[at, :], w[:, to], preferred_element_type=F32).astype(BF16)

        rest = units % wide
        if rest:
            to = pl.ds(units - rest, rest)
            acc[at, to] = jnp.dot(go[at, :], w[:, to], preferred_element_type=F32).astype(BF16)

    sides = (1 - xh, xh)
    order = (z, zm, zp, zf)

    def pfar_to(s, d):
        name, device = (("p_far_up", up_y), ("p_far_dn", dn_y))[d]
        send((name, s), acc.at[rows(sides[s], yf, d), rcols[0]], pfar.at[s, d], device, False)

    def pnear_to(s, d, h):
        name, b, device = (("p_up", yp, up_y), ("p_dn", ym, dn_y))[d]
        to = pnear.at[s, d, pl.ds(h * half, half)]
        send((name, s, h), acc.at[rows(sides[s], b, h), rcols[0]], to, device, False)

    def release(i):
        send(("q_x", i), acc.at[rows(1 - xh, order[i]), rcols[1]], qx.at[i], over_x)
        away = (order[i] - y + NY) % NY

        @pl.when(away == 2)
        def _():
            for s in (0, 1):
                pfar_to(s, 0)
                pfar_to(s, 1)

        @pl.when(away == 1)
        def _():
            for s in (0, 1):
                pnear_to(s, 0, 1)

        @pl.when(away == 3)
        def _():
            for s in (0, 1):
                pnear_to(s, 1, 0)

    for h in (0, 1):
        garrived("g_next", 1 - xl, z, c, h)
        gsend("g_xup", 1 - xl, z, c, up_z, h)
        gsend("g_xdn", 1 - xl, z, c, dn_z, h)
        gsend("g_xother", 1 - xl, z, c, other, h)
        if h == 0:
            harrived("h_up", xh, ym, 0, 0)
            hsend("h_up2", xh, ym, 0, up_y, 0)
            harrived("h_dn", xh, yp, 0, 1)
            hsend("h_dn2", xh, yp, 0, dn_y, 1)
    garrived("g_up", xl, zm, c, 0)
    gsend("g_up2", xl, zm, c, up_z, 0)
    garrived("g_dn", xl, zp, c, 1)
    gsend("g_dn2", xl, zp, c, dn_z, 1)
    garrived("g_up", xl, zm, c, 1)
    gsend("g_upo", xl, zm, c, other)
    garrived("g_dn", xl, zp, c, 0)
    gsend("g_dno", xl, zp, c, other)
    harrived("h_x", 1 - xh, y, 0, 0)
    hsend("h_gup", 1 - xh, y, 0, up_y, 0)
    hsend("h_gdn", 1 - xh, y, 0, dn_y, 0)
    harrived("h_up", xh, ym, 1, 0)
    hsend("h_up2", xh, ym, 1, up_y, 0)
    hsend("h_xm", xh, ym, 1, over_x, 0)
    harrived("h_dn", xh, yp, 1, 1)
    hsend("h_dn2", xh, yp, 1, dn_y, 1)
    hsend("h_xp", xh, yp, 1, over_x, 1)
    harrived("h_x", 1 - xh, y, 0, 1)
    hsend("h_gdn", 1 - xh, y, 0, dn_y, 1)
    hsend("h_gup", 1 - xh, y, 0, up_y, 1)
    harrived("h_up", xh, ym, 1, 1)
    hsend("h_xm", xh, ym, 1, over_x, 1)
    harrived("h_dn", xh, yp, 1, 0)
    hsend("h_xp", xh, yp, 1, over_x, 0)
    loads[4].wait()
    loads[5].wait()
    garrived("g_other", xl, z, 1 - c)
    garrived("g_xother", 1 - xl, z, 1 - c, 0)
    garrived("g_xother", 1 - xl, z, 1 - c, 1)
    project(z)
    garrived("g_xup", 1 - xl, zm, c, 0)
    gsend("g_xup2", 1 - xl, zm, c, up_z, 0)
    garrived("g_xdn", 1 - xl, zp, c, 1)
    gsend("g_xdn2", 1 - xl, zp, c, dn_z, 1)
    garrived("g_xup", 1 - xl, zm, c, 1)
    gsend("g_xupo", 1 - xl, zm, c, other)
    garrived("g_xdn", 1 - xl, zp, c, 0)
    gsend("g_xdno", 1 - xl, zp, c, other)
    garrived("g_upo", xl, zm, 1 - c)
    garrived("g_xupo", 1 - xl, zm, 1 - c)
    project(zm)
    harrived("h_gup", 1 - xh, ym, 0, 0)
    hsend("h_gup2", 1 - xh, ym, 0, up_y, 0)
    harrived("h_up2", xh, yf, 1, 0)
    hsend("h_xf", xh, yf, 1, over_x, 0)
    harrived("h_dn2", xh, yf, 1, 1)
    hsend("h_xf", xh, yf, 1, over_x, 1)
    harrived("h_gdn", 1 - xh, yp, 0, 1)
    hsend("h_gdn2", 1 - xh, yp, 0, dn_y, 1)
    release(0)
    release(1)
    garrived("g_up2", xl, zf, c, 0)
    garrived("g_dn2", xl, zf, c, 1)
    gsend("g_faro", xl, zf, c, other)
    garrived("g_dno", xl, zp, 1 - c)
    garrived("g_xdno", 1 - xl, zp, 1 - c)
    project(zp)
    release(2)
    garrived("g_xup2", 1 - xl, zf, c, 0)
    garrived("g_xdn2", 1 - xl, zf, c, 1)
    gsend("g_xfaro", 1 - xl, zf, c, other)
    garrived("g_faro", xl, zf, 1 - c)
    garrived("g_xfaro", 1 - xl, zf, 1 - c)
    project(zf)
    release(3)

    def add(at, p, ref):
        acc[at, rcols[p]] = (acc[at, rcols[p]].astype(F32) + ref[...].astype(F32)).astype(BF16)

    def meet(s):
        for d, (name, b) in enumerate((("p_far_up", yp), ("p_far_dn", ym))):
            arrived((name, s), pfar.at[s, d])
            add(rows(sides[s], b, d), 0, pfar.at[s, d])
            pnear_to(s, d, d)

    deep = features // 8

    def outer(f):
        at = pl.ds(f * deep, deep)
        gw[at, :] = lax.dot_general(
            go[:, at], hid[...], (((0,), (0,)), ((), ())), preferred_element_type=F32
        ).astype(BF16)

    def qadd(i):
        arrived(("q_x", i), qx.at[i])
        add(rows(xh, order[i]), 1, qx.at[i])

    def qfar_to(d):
        name, device = (("q_far_up", up_y), ("q_far_dn", dn_y))[d]
        send((name, 0), acc.at[rows(xh, yf, d), rcols[1]], qfar.at[d], device)

    def qnear_to(d, h):
        name, b, device = (("q_up", yp, up_y), ("q_dn", ym, dn_y))[d]
        send((name, h), acc.at[rows(xh, b, h), rcols[1]], qnear.at[d, pl.ds(h * half, half)], device)

    for h in (0, 1):
        harrived("h_x", 1 - xh, y, 1, h)
        harrived("h_xm", 1 - xh, ym, 1, h)
        harrived("h_xp", 1 - xh, yp, 1, h)
        harrived("h_xf", 1 - xh, yf, 1, h)
    harrived("h_up", xh, ym, 0, 1)
    harrived("h_dn", xh, yp, 0, 0)
    harrived("h_up2", xh, yf, 0, 0)
    harrived("h_dn2", xh, yf, 0, 1)
    harrived("h_gup", 1 - xh, ym, 0, 1)
    harrived("h_gdn", 1 - xh, yp, 0, 0)
    harrived("h_gup2", 1 - xh, yf, 0, 0)
    harrived("h_gdn2", 1 - xh, yf, 0, 1)
    def near_sum(s):
        for h in (0, 1):
            arrived(("p_up", s, h), pnear.at[s, 0, pl.ds(h * half, half)])
            arrived(("p_dn", s, h), pnear.at[s, 1, pl.ds(h * half, half)])

    outer(0)
    outer(1)
    outer(2)
    outer(3)
    meet(0)
    qadd(0)
    outer(4)
    qadd(1)
    meet(1)
    outer(5)
    qadd(2)
    outer(6)
    drain()
    for h in (0, 1):
        at, piece = rows(1 - xh, y, h), pl.ds(h * half, half)
        arrived(("p_up", 0, h), pnear.at[0, 0, piece])
        arrived(("p_dn", 0, h), pnear.at[0, 1, piece])
        total = acc[at, rcols[0]].astype(F32) + pnear[0, 0, piece].astype(F32) + pnear[0, 1, piece].astype(F32)
        acc[at, rcols[0]] = total.astype(BF16)
        send(("p_x", h), acc.at[at, rcols[0]], px.at[piece], over_x)
    qadd(3)
    for d in (0, 1):
        qfar_to(d)
    qnear_to(0, 1)
    qnear_to(1, 0)
    outer(7)
    for d, (name, b) in enumerate((("q_far_up", yp), ("q_far_dn", ym))):
        arrived((name, 0), qfar.at[d])
        add(rows(xh, b, d), 1, qfar.at[d])
        qnear_to(d, d)

    def finish(p, piece, total):
        gu[piece, rcols[p]] = (total * silu[piece, rcols[p]]).astype(BF16)
        gg[piece, rcols[p]] = (total * slope[piece, rcols[p]]).astype(BF16)

    near_sum(1)
    for h in (0, 1):
        piece = pl.ds(h * half, half)
        arrived(("p_x", h), px.at[piece])
        total = acc[rows(xh, y, h), rcols[0]].astype(F32) + px[piece].astype(F32)
        total = total + pnear[1, 0, piece].astype(F32) + pnear[1, 1, piece].astype(F32)
        finish(0, piece, total)
    for s in (0, 1):
        sent["p_far_up", s], sent["p_far_dn", s] = pfar.at[s, 0], pfar.at[s, 1]
        for h in (0, 1):
            sent["p_up", s, h] = sent["p_dn", s, h] = pnear.at[s, 0, pl.ds(h * half, half)]
    drain()
    for h in (0, 1):
        piece = pl.ds(h * half, half)
        arrived(("q_up", h), qnear.at[0, piece])
        arrived(("q_dn", h), qnear.at[1, piece])
        total = acc[rows(xh, y, h), rcols[1]].astype(F32)
        total = total + qnear[0, piece].astype(F32) + qnear[1, piece].astype(F32)
        finish(1, piece, total)


def emit(gg_in, gu_in, gw_in, gg_out, gu_out, gw_out, sems):
    pieces = 8
    deep = gw_in.shape[0] // pieces
    copies = [pltpu.make_async_copy(gg_in, gg_out, sems.at[pieces]), pltpu.make_async_copy(gu_in, gu_out, sems.at[pieces + 1])]
    for i in range(pieces):
        at = pl.ds(i * deep, deep)
        copies.append(pltpu.make_async_copy(gw_in.at[at], gw_out.at[at], sems.at[i]))
    for copy in copies:
        copy.start()
    for copy in copies:
        copy.wait()


def on_device(grad_out, gate, up, w_down):
    own, units = gate.shape
    features = w_down.shape[0]
    tokens = own * NX * NY
    hsplit, split = 1024, 1024
    rest = units - split
    half = own // 2
    anywhere = pl.BlockSpec(memory_space=pl.ANY)
    results = pl.pallas_call(
        functools.partial(kernel, hsplit, split),
        out_shape=(
            jax.ShapeDtypeStruct((own, units), BF16),
            jax.ShapeDtypeStruct((own, units), BF16),
            jax.ShapeDtypeStruct((features, units), BF16),
        ),
        in_specs=[anywhere] * 4,
        out_specs=(pl.BlockSpec(memory_space=pltpu.VMEM),) * 3,
        scratch_shapes=[
            pltpu.VMEM((tokens, features), BF16),
            pltpu.VMEM((features, units), BF16),
            pltpu.VMEM((tokens, units), BF16),
            pltpu.VMEM((tokens, units), BF16),
            pltpu.VMEM((own, units), BF16),
            pltpu.VMEM((own, units), BF16),
            pltpu.VMEM((own, units), F32),
            pltpu.VMEM((own, units), F32),
            pltpu.VMEM((2, 2, half, split), BF16),
            pltpu.VMEM((2, 2, own, split), BF16),
            pltpu.VMEM((own, split), BF16),
            pltpu.VMEM((NY, own, rest), BF16),
            pltpu.VMEM((2, half, rest), BF16),
            pltpu.VMEM((2, own, rest), BF16),
            pltpu.SemaphoreType.DMA((6,)),
            pltpu.SemaphoreType.DMA((COPIES,)),
            pltpu.SemaphoreType.DMA((COPIES,)),
        ],
        compiler_params=pltpu.CompilerParams(
            collective_id=0, has_side_effects=True, vmem_limit_bytes=40 * 2**20
        ),
        cost_estimate=pl.CostEstimate(
            flops=4 * tokens * features * units, bytes_accessed=4 * features * units, transcendentals=own * units
        ),
    )(*[pltpu.with_memory_space_constraint(a, pltpu.HBM) for a in (grad_out, gate, up, w_down)])
    return pl.pallas_call(
        emit,
        out_shape=tuple(jax.ShapeDtypeStruct(r.shape, r.dtype) for r in results),
        in_specs=[pl.BlockSpec(memory_space=pl.ANY)] * 3,
        out_specs=(pl.BlockSpec(memory_space=pltpu.HBM),) * 3,
        scratch_shapes=[pltpu.SemaphoreType.DMA((10,))],
        compiler_params=pltpu.CompilerParams(vmem_limit_bytes=4 * 2**20),
    )(*[pltpu.with_memory_space_constraint(r, pltpu.VMEM) for r in results])


def solution(mesh):
    return jax.shard_map(
        on_device,
        mesh=mesh,
        in_specs=(P("col", "row"), P("row", "col"), P("row", "col"), P("row", "col")),
        out_specs=(P("row", "col"),) * 3,
        check_vma=False,
    )
```
